32 devices in a mesh: film: 2 (over y), tm: 4 (over z), rows: 2 (over x), cols: 2 (over core).
Axes of the slice: x: 2, y: 2, z: 4, core: 2. Of those that a mesh axis runs over, the one named last changes fastest.
Arguments:
- noisy_luma: float32 [32, 256, 1536], P(('film', 'tm'), 'rows', 'cols'), parts along dimension 0, may hold values from -6 to 6
- scene_cuts: int32 [6], P('film'), parts along dimension 0, may hold values from 1 to 15
Outputs:
- denoised: float32 [32, 256, 1536], P(('film', 'tm'), 'rows', 'cols'), parts along dimension 0
The draws below stay inside these ranges and needn't reach their ends.
There are 2 independent parts, one for each index of `film`. The reference program is written for one: setup_inputs(seed, part) draws one part's arguments, and reference() takes and returns one part's arrays. A program takes and returns all parts, laid end to end along the dimension named above; each array names one. Nothing has to cross between parts.
All inputs are finite; a program needn't handle non-finite values.
Results may differ from the reference program's by a relative error of at most 0.00002.
Values sent between devices are 32-bit elements; how exact they have to be, the bound alone decides.
A program may use at most 64 MiB of HBM per device.

```python
import jax
import jax.numpy as jnp
from jax import lax

ITERS = 4
NCUT = 3
FRAMES = 16
HEIGHT = 256
WIDTH = 1536


def steps_of(rng, shape, split, low, largest):
    level = 1.0
    for axis_at, parts in split:
        steps = jax.random.uniform(jax.random.fold_in(jax.random.fold_in(rng, 6), axis_at), (parts,), jnp.float32, low / len(split), largest / len(split))
        level = level * jnp.repeat(jnp.exp(steps), shape[axis_at] // parts).reshape((-1,) + (1,) * (len(shape) - 1 - axis_at))
    return level


def centred(own_key, shape, width, reach, cuts=(), held_as=jnp.bfloat16):
    drawn = width * jax.random.normal(own_key, shape, jnp.float32)
    if cuts:
        drawn = drawn * steps_of(own_key, shape, cuts, -0.22, 0.18)
    return jnp.clip(drawn, -reach, reach).astype(held_as)


def setup_inputs(seed: int = 0, part: int = 0) -> dict:
    key_list = jax.random.split(jax.random.key(seed), 3)
    part_splits = jax.random.split(jax.random.fold_in(key_list[2], part), 3)
    return {
        "noisy_luma": centred(part_splits[0], (FRAMES, HEIGHT, WIDTH), 1.0, 6.0, ((0, 4), (1, 2), (2, 2)), jnp.float32),
        "scene_cuts": jax.random.randint(part_splits[1], (NCUT,), 1, FRAMES).astype(jnp.int32),
    }


dual_step = 12.0 ** (-0.5)
primal_step = 12.0 ** (-0.5)
radius = 0.6

def forward(values, along):
    padding = [(0, 0), (0, 0), (0, 0)]
    padding[along] = (0, 1)
    padded = jnp.pad(values, padding)
    return lax.slice_in_dim(padded, 1, padded.shape[along], axis=along)

def backward(values, along):
    padding = [(0, 0), (0, 0), (0, 0)]
    padding[along] = (1, 0)
    padded = jnp.pad(values, padding)
    return lax.slice_in_dim(padded, 0, padded.shape[along] - 1, axis=along)

def make_masks(scene_cuts, offset, length, extent, temporal):
    indices = offset + jnp.arange(length, dtype=jnp.int32)
    inside = (indices >= 0) & (indices <= extent - 2)
    if temporal:
        struck = jnp.any(scene_cuts[None, :] == indices[:, None] + 1, axis=1)
        inside = inside & jnp.logical_not(struck)
    return inside.astype(jnp.float32)

def gradient(values, mask_t, mask_h, mask_w):
    slope_t = (forward(values, 0) - values) * mask_t[:, None, None]
    slope_h = (forward(values, 1) - values) * mask_h[None, :, None]
    slope_w = (forward(values, 2) - values) * mask_w[None, None, :]
    return (slope_t, slope_h, slope_w)

def divergence(dual_t, dual_h, dual_w):
    return dual_t - backward(dual_t, 0) + (dual_h - backward(dual_h, 1)) + (dual_w - backward(dual_w, 2))

def project(dual_parts, slopes):
    stepped = [previous + dual_step * slope for previous, slope in zip(dual_parts, slopes)]
    magnitude = jnp.sqrt(stepped[0] * stepped[0] + stepped[1] * stepped[1] + stepped[2] * stepped[2])
    shrink = 1.0 / jnp.maximum(1.0, magnitude / radius)
    return (stepped[0] * shrink, stepped[1] * shrink, stepped[2] * shrink)

def primal_update(current, diverged, noisy_luma):
    return (current + primal_step * diverged + primal_step * noisy_luma) / (1.0 + primal_step)

def reference(noisy_luma, scene_cuts):
    frames, height, breadth = noisy_luma.shape
    mask_t = make_masks(scene_cuts, 0, frames, frames, True)
    mask_h = make_masks(scene_cuts, 0, height, height, False)
    mask_w = make_masks(scene_cuts, 0, breadth, breadth, False)
    current = noisy_luma
    relaxed = noisy_luma
    zeroes = jnp.zeros_like(noisy_luma)
    dual_parts = (zeroes, zeroes, zeroes)
    for sweep in range(ITERS):
        slopes = gradient(relaxed, mask_t, mask_h, mask_w)
        dual_parts = project(dual_parts, slopes)
        updated = primal_update(current, divergence(*dual_parts), noisy_luma)
        relaxed = 2.0 * updated - current
        current = updated
    return current
```

```python
import functools

import jax
import jax.numpy as jnp
from jax import lax
from jax.experimental import pallas as pl
from jax.experimental.pallas import tpu as pltpu
from jax.sharding import PartitionSpec as P

MESH = pl.DeviceIdType.MESH

dual_step = 12.0 ** (-0.5)
primal_step = 12.0 ** (-0.5)
radius = 0.6

reach = radius / dual_step
keep = 1.0 / (1.0 + primal_step)
push = primal_step * dual_step / (1.0 + primal_step)
pull = primal_step / (1.0 + primal_step)

TILE = 8
LANES = 128


def kernel(tm_size, row_size, x, cuts, out, noisy, relaxed, far, current, dual_t, dual_h, dual_w,
           mask_w, load_sem, z_send, z_recv, r_send, r_recv, c_send, c_recv, out_sem):
    frames, rows, cols = x.shape
    high = rows + 2 * TILE
    wide = cols + LANES
    tiles = high // TILE
    tm = lax.axis_index("tm")
    band = lax.axis_index("rows")
    core = lax.axis_index("cols")
    has_left = tm > 0
    has_right = tm < tm_size - 1
    up = lax.rem(band + row_size - 1, row_size)
    down = lax.rem(band + 1, row_size)
    other = 1 - core
    own_rows = pl.ds(TILE, rows)
    own_cols = pl.ds(0, cols)

    def far_slot(level, side):
        return 2 * (level - 1) + side

    def at(level, t):
        if level == 0:
            return noisy.at[t + 2]
        if -1 <= t <= frames:
            return relaxed.at[level - 1, t + 1]
        return far.at[far_slot(level, 0 if t < 0 else 1)]

    def greet(device):
        pl.semaphore_signal(barrier, inc=1, device_id=device, device_id_type=MESH)

    barrier = pltpu.get_barrier_semaphore()
    greet({"rows": up})
    greet({"rows": down})
    greet({"cols": other})

    @pl.when(has_left)
    def _():
        greet({"tm": tm - 1})

    @pl.when(has_right)
    def _():
        greet({"tm": tm + 1})

    load = pltpu.make_async_copy(x, noisy.at[pl.ds(2, frames), own_rows, own_cols], load_sem)
    load.start()
    pl.semaphore_wait(barrier, 3 + has_left.astype(jnp.int32) + has_right.astype(jnp.int32))

    def along_tm(stage):
        if stage == 0:
            ends = (x.at[0], at(0, frames)), (x.at[frames - 1], at(0, -1))
        elif stage == 1:
            ends = (x.at[1], at(0, frames + 1)), (x.at[frames - 2], at(0, -2))
        else:
            level = stage - 1
            ends = (
                (at(level, 1).at[own_rows, own_cols], at(level, frames + 1)),
                (at(level, frames - 2).at[own_rows, own_cols], at(level, -2)),
            )
        return [
            pltpu.make_async_remote_copy(
                src_ref=source,
                dst_ref=target.at[own_rows, own_cols],
                send_sem=z_send.at[stage, side],
                recv_sem=z_recv.at[stage, side],
                device_id={"tm": tm - 1 if side == 0 else tm + 1},
                device_id_type=MESH,
            )
            for side, (source, target) in enumerate(ends)
        ]

    def send_frames(stage):
        left, right = along_tm(stage)
        pl.when(has_left)(left.start)
        pl.when(has_right)(right.start)

    def await_frames(stage):
        left, right = along_tm(stage)
        pl.when(has_right)(left.wait_recv)
        pl.when(has_left)(right.wait_recv)

    def await_sent(stage):
        left, right = along_tm(stage)
        pl.when(has_left)(left.wait_send)
        pl.when(has_right)(right.wait_send)

    def arrived(stage):
        if stage == 0:
            return at(0, frames), at(0, -1)
        if stage == 1:
            return at(0, frames + 1), at(0, -2)
        return at(stage - 1, frames + 1), at(stage - 1, -2)

    def row_halo(slot, source, target):
        first, last = source
        return [
            pltpu.make_async_remote_copy(
                src_ref=first, dst_ref=target[1], send_sem=r_send.at[slot, 0], recv_sem=r_recv.at[slot, 0],
                device_id={"rows": up}, device_id_type=MESH),
            pltpu.make_async_remote_copy(
                src_ref=last, dst_ref=target[0], send_sem=r_send.at[slot, 1], recv_sem=r_recv.at[slot, 1],
                device_id={"rows": down}, device_id_type=MESH),
        ]

    edge = pl.ds(pl.multiple_of(other * (cols - LANES), LANES), LANES)

    def col_halo(slot, source, target):
        return pltpu.make_async_remote_copy(
            src_ref=source, dst_ref=target, send_sem=c_send.at[slot], recv_sem=c_recv.at[slot],
            device_id={"cols": other}, device_id_type=MESH)

    above, below = pl.ds(0, TILE), pl.ds(TILE + rows, TILE)
    all_rows, beyond = pl.ds(0, high), pl.ds(cols, LANES)
    own = pl.ds(2, frames)
    own_row_halo = row_halo(
        0,
        (x.at[:, pl.ds(0, TILE)], x.at[:, pl.ds(rows - TILE, TILE)]),
        (noisy.at[own, above, own_cols], noisy.at[own, below, own_cols]),
    )
    own_col_halo = col_halo(0, noisy.at[own, all_rows, edge], noisy.at[own, all_rows, beyond])

    def row_halos(stage):
        copies = []
        for side, frame in enumerate(arrived(stage)):
            copies += row_halo(
                1 + 2 * stage + side,
                (frame.at[pl.ds(TILE, TILE), own_cols], frame.at[pl.ds(rows, TILE), own_cols]),
                (frame.at[above, own_cols], frame.at[below, own_cols]),
            )
        return copies

    def col_halos(stage):
        return [
            col_halo(1 + 2 * stage + side, frame.at[all_rows, edge], frame.at[all_rows, beyond])
            for side, frame in enumerate(arrived(stage))
        ]

    sub = lax.broadcasted_iota(jnp.int32, (TILE, LANES), 0)
    spread = lambda v: jnp.concatenate([v] * (wide // LANES), axis=1)
    first_row = spread(sub) == 0
    last_row = spread(sub) == TILE - 1
    above_open = band > 0
    below_open = band < row_size - 1

    total_frames = frames * tm_size

    def frame_mask(t):
        g = tm * frames + t
        open_ = (g >= 0) & (g <= total_frames - 2)
        for j in range(cuts.shape[0]):
            open_ = open_ & (cuts[j] != g + 1)
        return jnp.where(open_, 1.0, 0.0).astype(jnp.float32)

    def dual(level, t):
        here, after = at(level - 1, t), at(level - 1, t + 1)
        mask_t = frame_mask(t)

        def step(i, _):
            r = pl.ds(pl.multiple_of(i * TILE, TILE), TILE)
            n = pl.ds(pl.multiple_of(jnp.minimum(i + 1, tiles - 1) * TILE, TILE), TILE)
            v = here[r, :]
            row = sub + i * TILE
            shut = ((row == TILE - 1) & jnp.logical_not(above_open)) | (
                (row == TILE + rows - 1) & jnp.logical_not(below_open))
            mask_h = spread(jnp.where(shut, 0.0, 1.0).astype(jnp.float32))
            a = (after[r, :] - v) * mask_t
            b = (pltpu.roll(jnp.where(first_row, here[n, :], v), TILE - 1, 0) - v) * mask_h
            c = (pltpu.roll(v, wide - 1, 1) - v) * mask_w[...]
            if level > 1:
                a = a + dual_t[t + 2, r, :]
                b = b + dual_h[t + 2, r, :]
                c = c + dual_w[t + 2, r, :]
            shrink = jnp.minimum(1.0, reach * lax.rsqrt(a * a + b * b + c * c))
            dual_t[t + 2, r, :] = a * shrink
            dual_h[t + 2, r, :] = b * shrink
            dual_w[t + 2, r, :] = c * shrink
            return 0

        lax.fori_loop(0, tiles, step, 0)

    def primal(level, t):
        held = current.at[t + 1]
        before = noisy.at[t + 2] if level == 1 else held
        start = noisy.at[t + 2]

        def step(i, _):
            r = pl.ds(pl.multiple_of(i * TILE, TILE), TILE)
            p = pl.ds(pl.multiple_of(jnp.maximum(i - 1, 0) * TILE, TILE), TILE)
            h = dual_h[t + 2, r, :]
            w = dual_w[t + 2, r, :]
            gone = dual_t[t + 2, r, :] - dual_t[t + 1, r, :]
            gone = gone + (h - pltpu.roll(jnp.where(last_row, dual_h[t + 2, p, :], h), 1, 0))
            gone = gone + (w - pltpu.roll(w, 1, 1))
            old = before[r, :]
            new = keep * old + push * gone + pull * start[r, :]
            held[r, :] = new
            if level < 4:
                at(level, t)[r, :] = 2.0 * new - old
            return 0

        lax.fori_loop(0, tiles, step, 0)

    def finish(t):
        return pltpu.make_async_copy(current.at[t + 1, own_rows, own_cols], out.at[t], out_sem.at[t])

    for copy in own_row_halo:
        copy.start()
    send_frames(0)
    lane = lax.broadcasted_iota(jnp.int32, (TILE, wide), 1)
    mask_w[...] = jnp.where(lane == jnp.where(core == 0, wide - 1, cols - 1), 0.0, 1.0).astype(jnp.float32)

    def clear(refs):
        def step(i, _):
            r = pl.ds(pl.multiple_of(i * TILE, TILE), TILE)
            for ref in refs:
                ref[r, :] = jnp.zeros((TILE, wide), jnp.float32)
            return 0

        lax.fori_loop(1, tiles - 1, step, 0)

    @pl.when(jnp.logical_not(has_left))
    def _():
        clear([at(0, -1), at(0, -2), at(1, -2), at(2, -2)])

    @pl.when(jnp.logical_not(has_right))
    def _():
        clear([at(0, frames), at(0, frames + 1), at(1, frames + 1), at(2, frames + 1)])

    load.wait()
    for copy in own_row_halo:
        copy.wait_recv()
    own_col_halo.start()
    own_col_halo.wait_recv()

    def receive(stage):
        await_frames(stage)
        rows_in = row_halos(stage)
        for copy in rows_in:
            copy.start()
        if stage == 0:
            send_frames(1)
        for copy in rows_in:
            copy.wait_recv()
        cols_in = col_halos(stage)
        for copy in cols_in:
            copy.start()
        for copy in cols_in:
            copy.wait_recv()

    dual(1, 0)
    dual(1, 1)
    primal(1, 1)
    dual(1, 2)
    primal(1, 2)
    dual(2, 1)
    receive(0)

    dual(1, -1)
    primal(1, 0)
    dual(1, 3)
    primal(1, 3)
    dual(2, 0)
    primal(2, 1)
    dual(2, 2)
    primal(2, 2)
    send_frames(2)
    dual(3, 1)
    receive(1)

    dual(1, -2)
    primal(1, -1)
    dual(1, 4)
    primal(1, 4)
    dual(2, -1)
    primal(2, 0)
    dual(2, 3)
    primal(2, 3)
    send_frames(3)
    dual(3, 0)
    primal(3, 1)
    dual(3, 2)
    primal(3, 2)
    dual(4, 1)
    receive(2)

    dual(2, -2)
    primal(2, -1)
    dual(2, 4)
    primal(2, 4)
    dual(3, -1)
    primal(3, 0)
    dual(3, 3)
    primal(3, 3)
    dual(4, 0)
    primal(4, 1)
    finish(1).start()
    dual(4, 2)
    primal(4, 2)
    finish(2).start()
    receive(3)

    dual(3, -2)
    primal(3, -1)
    dual(4, -1)
    primal(4, 0)
    finish(0).start()
    dual(3, 4)
    primal(3, 4)
    dual(4, 3)
    primal(4, 3)
    finish(3).start()

    for stage in range(4):
        await_sent(stage)
        for copy in row_halos(stage) + col_halos(stage):
            copy.wait_send()
    for copy in own_row_halo + [own_col_halo]:
        copy.wait_send()
    for t in range(frames):
        finish(t).wait()


def solution(mesh):
    tm_size, row_size = mesh.shape["tm"], mesh.shape["rows"]

    def body(noisy_luma, scene_cuts):
        frames, rows, cols = noisy_luma.shape
        field = (rows + 2 * TILE, cols + LANES)
        buffer = lambda *lead: pltpu.VMEM(lead + field, jnp.float32)
        dma = pltpu.SemaphoreType.DMA
        return pl.pallas_call(
            functools.partial(kernel, tm_size, row_size),
            out_shape=jax.ShapeDtypeStruct(noisy_luma.shape, jnp.float32),
            in_specs=[pl.BlockSpec(memory_space=pl.ANY), pl.BlockSpec(memory_space=pltpu.SMEM)],
            out_specs=pl.BlockSpec(memory_space=pl.ANY),
            scratch_shapes=[
                buffer(frames + 4),
                buffer(3, frames + 2),
                buffer(4),
                buffer(frames + 2),
                buffer(frames + 3),
                buffer(frames + 3),
                buffer(frames + 3),
                pltpu.VMEM((TILE, cols + LANES), jnp.float32),
                dma(()),
                dma((4, 2)),
                dma((4, 2)),
                dma((9, 2)),
                dma((9, 2)),
                dma((9,)),
                dma((9,)),
                dma((frames,)),
            ],
            compiler_params=pltpu.CompilerParams(
                collective_id=0, has_side_effects=True, vmem_limit_bytes=48 * 1024 * 1024),
        )(noisy_luma, scene_cuts)

    return jax.shard_map(
        body,
        mesh=mesh,
        in_specs=(P(("film", "tm"), "rows", "cols"), P("film")),
        out_specs=P(("film", "tm"), "rows", "cols"),
        check_vma=False,
    )
```

```python
import functools

import jax
import jax.numpy as jnp
from jax import lax
from jax.experimental import pallas as pl
from jax.experimental.pallas import tpu as pltpu
from jax.sharding import PartitionSpec as P

MESH = pl.DeviceIdType.MESH

dual_step = 12.0 ** (-0.5)
primal_step = 12.0 ** (-0.5)
radius = 0.6

reach = radius / dual_step
keep = 1.0 / (1.0 + primal_step)
push = primal_step * dual_step / (1.0 + primal_step)
pull = primal_step / (1.0 + primal_step)

TILE = 8
LANES = 128
DEEP = 4


def kernel(tm_size, row_size, x, cuts, out, noisy, relaxed, far, current, dual_t, dual_h, dual_w,
           mask_h, mask_w, load_sem, z_send, z_recv, h_send, h_recv, out_sem):
    frames, rows, cols = x.shape
    high = rows + TILE
    wide = cols + LANES
    tm = lax.axis_index("tm")
    band = lax.axis_index("rows")
    core = lax.axis_index("cols")
    has_left = tm > 0
    has_right = tm < tm_size - 1
    has_up = band > 0
    has_down = band < row_size - 1
    other = 1 - core
    own_rows = pl.ds(0, rows)
    own_cols = pl.ds(0, cols)

    def at(level, t):
        if level == 0:
            return noisy.at[t + 2]
        if -1 <= t <= frames:
            return relaxed.at[level - 1, t + 1]
        return far.at[2 * (level - 1) + (0 if t < 0 else 1)]

    for ref in (noisy, far):
        for f in range(ref.shape[0]):
            ref[f, rows:high, :] = jnp.zeros((TILE, wide), jnp.float32)

    barrier = pltpu.get_barrier_semaphore()

    def greet(device):
        pl.semaphore_signal(barrier, inc=1, device_id=device, device_id_type=MESH)

    greet({"cols": other})

    @pl.when(has_up)
    def _():
        greet({"rows": band - 1})
        greet({"rows": band - 1, "cols": other})

    @pl.when(has_down)
    def _():
        greet({"rows": band + 1})
        greet({"rows": band + 1, "cols": other})

    @pl.when(has_left)
    def _():
        greet({"tm": tm - 1})

    @pl.when(has_right)
    def _():
        greet({"tm": tm + 1})

    load = pltpu.make_async_copy(x, noisy.at[pl.ds(2, frames), own_rows, own_cols], load_sem)
    load.start()
    count = lambda flag: flag.astype(jnp.int32)
    pl.semaphore_wait(barrier, 1 + 2 * count(has_up) + 2 * count(has_down) + count(has_left) + count(has_right))

    def along_tm(stage):
        if stage == 0:
            ends = (x.at[0], at(0, frames)), (x.at[frames - 1], at(0, -1))
        elif stage == 1:
            ends = (x.at[1], at(0, frames + 1)), (x.at[frames - 2], at(0, -2))
        else:
            level = stage - 1
            ends = (
                (at(level, 1).at[own_rows, own_cols], at(level, frames + 1)),
                (at(level, frames - 2).at[own_rows, own_cols], at(level, -2)),
            )
        return [
            pltpu.make_async_remote_copy(
                src_ref=source,
                dst_ref=target.at[own_rows, own_cols],
                send_sem=z_send.at[stage, side],
                recv_sem=z_recv.at[stage, side],
                device_id={"tm": tm - 1 if side == 0 else tm + 1},
                device_id_type=MESH,
            )
            for side, (source, target) in enumerate(ends)
        ]

    def send_frames(stage):
        left, right = along_tm(stage)
        pl.when(has_left)(left.start)
        pl.when(has_right)(right.start)

    def await_frames(stage):
        left, right = along_tm(stage)
        pl.when(has_right)(left.wait_recv)
        pl.when(has_left)(right.wait_recv)

    def await_sent(stage):
        left, right = along_tm(stage)
        pl.when(has_left)(left.wait_send)
        pl.when(has_right)(right.wait_send)

    edge = pl.ds(pl.multiple_of(other * (cols - LANES), LANES), LANES)
    beyond = pl.ds(cols, LANES)
    below, above = pl.ds(rows, DEEP), pl.ds(rows + DEEP, DEEP)
    first, last = pl.ds(0, DEEP), pl.ds(rows - DEEP, DEEP)

    def halo(slot, source, target, lead=()):
        def copy(n, src, dst, device):
            return pltpu.make_async_remote_copy(
                src_ref=source.at[lead_src + src], dst_ref=target.at[lead + dst],
                send_sem=h_send.at[slot, n], recv_sem=h_recv.at[slot, n],
                device_id=device, device_id_type=MESH)

        lead_src = (slice(None),) if lead else ()
        ups = [
            copy(0, (first, own_cols), (below, own_cols), {"rows": band - 1}),
            copy(1, (first, edge), (below, beyond), {"rows": band - 1, "cols": other}),
        ]
        downs = [
            copy(2, (last, own_cols), (above, own_cols), {"rows": band + 1}),
            copy(3, (last, edge), (above, beyond), {"rows": band + 1, "cols": other}),
        ]
        side = copy(4, (own_rows, edge), (own_rows, beyond), {"cols": other})
        return ups, downs, side

    def halo_start(copies):
        ups, downs, side = copies
        side.start()

        @pl.when(has_up)
        def _():
            for c in ups:
                c.start()

        @pl.when(has_down)
        def _():
            for c in downs:
                c.start()

    def halo_wait_recv(copies):
        ups, downs, side = copies
        side.wait_recv()

        @pl.when(has_down)
        def _():
            for c in ups:
                c.wait_recv()

        @pl.when(has_up)
        def _():
            for c in downs:
                c.wait_recv()

    def halo_wait_send(copies):
        ups, downs, side = copies
        side.wait_send()

        @pl.when(has_up)
        def _():
            for c in ups:
                c.wait_send()

        @pl.when(has_down)
        def _():
            for c in downs:
                c.wait_send()

    own_halo = halo(0, x, noisy, (pl.ds(2, frames),))

    def halos(stage):
        if stage == 0:
            arrived = at(0, frames), at(0, -1)
        elif stage == 1:
            arrived = at(0, frames + 1), at(0, -2)
        else:
            arrived = at(stage - 1, frames + 1), at(stage - 1, -2)
        return [halo(1 + 2 * stage + side, frame, frame) for side, frame in enumerate(arrived)]

    total_frames = frames * tm_size

    def frame_mask(t):
        g = tm * frames + t
        open_ = (g >= 0) & (g <= total_frames - 2)
        for j in range(cuts.shape[0]):
            open_ = open_ & (cuts[j] != g + 1)
        return jnp.where(open_, 1.0, 0.0).astype(jnp.float32)

    frame_masks = {t: frame_mask(t) for t in range(-2, frames + 1)}
    sub = lax.broadcasted_iota(jnp.int32, (TILE, wide), 0)
    first_row = sub == 0
    last_row = sub == TILE - 1

    def dual(level, t):
        here, after = at(level - 1, t), at(level - 1, t + 1)
        for i in range(0, high, TILE):
            r, n = pl.ds(i, TILE), pl.ds((i + TILE) % high, TILE)
            v = here[r, :]
            a = (after[r, :] - v) * frame_masks[t]
            b = pltpu.roll(jnp.where(first_row, here[n, :], v), TILE - 1, 0) - v
            if i >= rows - TILE:
                b = b * mask_h[pl.ds(i - rows + TILE, TILE), :]
            c = (pltpu.roll(v, wide - 1, 1) - v) * mask_w[...]
            if level > 1:
                a = a + dual_t[t + 2, r, :]
                b = b + dual_h[t + 2, r, :]
                c = c + dual_w[t + 2, r, :]
            shrink = jnp.minimum(1.0, reach * lax.rsqrt(a * a + b * b + c * c))
            dual_t[t + 2, r, :] = a * shrink
            dual_h[t + 2, r, :] = b * shrink
            dual_w[t + 2, r, :] = c * shrink

    def primal(level, t):
        held = current.at[t + 1]
        start = noisy.at[t + 2]
        before = start if level == 1 else held
        for i in range(0, rows if level == 4 else high, TILE):
            r, p = pl.ds(i, TILE), pl.ds((i - TILE) % high, TILE)
            h = dual_h[t + 2, r, :]
            w = dual_w[t + 2, r, :]
            gone = dual_t[t + 2, r, :] - dual_t[t + 1, r, :]
            gone = gone + (h - pltpu.roll(jnp.where(last_row, dual_h[t + 2, p, :], h), 1, 0))
            gone = gone + (w - pltpu.roll(w, 1, 1))
            old = before[r, :]
            new = keep * old + push * gone + pull * start[r, :]
            held[r, :] = new
            if level < 4:
                at(level, t)[r, :] = 2.0 * new - old

    def finish(t):
        return pltpu.make_async_copy(current.at[t + 1, own_rows, own_cols], out.at[t], out_sem.at[t])

    send_frames(0)
    halo_start(own_halo)
    lane = lax.broadcasted_iota(jnp.int32, (TILE, wide), 1)
    mask_w[...] = jnp.where(lane == jnp.where(core == 0, wide - 1, cols - 1), 0.0, 1.0).astype(jnp.float32)
    mask_h[0:TILE, :] = jnp.where(last_row & jnp.logical_not(has_down), 0.0, 1.0).astype(jnp.float32)
    mask_h[TILE : 2 * TILE, :] = jnp.where(last_row & jnp.logical_not(has_up), 0.0, 1.0).astype(jnp.float32)

    def clear(refs):
        def step(i, _):
            r = pl.ds(pl.multiple_of(i * TILE, TILE), TILE)
            for ref in refs:
                ref[r, own_cols] = jnp.zeros((TILE, cols), jnp.float32)
            return 0

        lax.fori_loop(0, rows // TILE, step, 0)

    @pl.when(jnp.logical_not(has_left))
    def _():
        clear([at(0, -1), at(0, -2), at(1, -2), at(2, -2)])

    @pl.when(jnp.logical_not(has_right))
    def _():
        clear([at(0, frames), at(0, frames + 1), at(1, frames + 1), at(2, frames + 1)])

    load.wait()
    halo_wait_recv(own_halo)

    def forward(stage):
        await_frames(stage)
        for copies in halos(stage):
            halo_start(copies)

    def receive(stage):
        for copies in halos(stage):
            halo_wait_recv(copies)

    dual(1, 0)
    dual(1, 1)
    primal(1, 1)
    dual(1, 2)
    primal(1, 2)
    forward(0)
    send_frames(1)
    dual(2, 1)
    receive(0)

    dual(1, -1)
    primal(1, 0)
    dual(1, 3)
    primal(1, 3)
    dual(2, 0)
    primal(2, 1)
    dual(2, 2)
    primal(2, 2)
    send_frames(2)
    forward(1)
    dual(3, 1)
    receive(1)

    dual(1, -2)
    primal(1, -1)
    dual(1, 4)
    primal(1, 4)
    dual(2, -1)
    primal(2, 0)
    dual(2, 3)
    primal(2, 3)
    send_frames(3)
    dual(3, 0)
    primal(3, 1)
    dual(3, 2)
    primal(3, 2)
    forward(2)
    dual(4, 1)
    receive(2)

    dual(2, -2)
    primal(2, -1)
    dual(2, 4)
    primal(2, 4)
    dual(3, -1)
    primal(3, 0)
    dual(3, 3)
    primal(3, 3)
    dual(4, 0)
    primal(4, 1)
    finish(1).start()
    forward(3)
    dual(4, 2)
    primal(4, 2)
    finish(2).start()
    receive(3)

    dual(3, -2)
    primal(3, -1)
    dual(4, -1)
    primal(4, 0)
    finish(0).start()
    dual(3, 4)
    primal(3, 4)
    dual(4, 3)
    primal(4, 3)
    finish(3).start()

    for stage in range(4):
        await_sent(stage)
        for copies in halos(stage):
            halo_wait_send(copies)
    halo_wait_send(own_halo)
    for t in range(frames):
        finish(t).wait()


def solution(mesh):
    tm_size, row_size = mesh.shape["tm"], mesh.shape["rows"]

    def body(noisy_luma, scene_cuts):
        frames, rows, cols = noisy_luma.shape
        field = (rows + TILE, cols + LANES)
        buffer = lambda *lead: pltpu.VMEM(lead + field, jnp.float32)
        dma = pltpu.SemaphoreType.DMA
        return pl.pallas_call(
            functools.partial(kernel, tm_size, row_size),
            out_shape=jax.ShapeDtypeStruct(noisy_luma.shape, jnp.float32),
            in_specs=[pl.BlockSpec(memory_space=pl.ANY), pl.BlockSpec(memory_space=pltpu.SMEM)],
            out_specs=pl.BlockSpec(memory_space=pl.ANY),
            scratch_shapes=[
                buffer(frames + 4),
                buffer(3, frames + 2),
                buffer(4),
                buffer(frames + 2),
                buffer(frames + 3),
                buffer(frames + 3),
                buffer(frames + 3),
                pltpu.VMEM((2 * TILE, cols + LANES), jnp.float32),
                pltpu.VMEM((TILE, cols + LANES), jnp.float32),
                dma(()),
                dma((4, 2)),
                dma((4, 2)),
                dma((9, 5)),
                dma((9, 5)),
                dma((frames,)),
            ],
            compiler_params=pltpu.CompilerParams(
                collective_id=0, has_side_effects=True, vmem_limit_bytes=48 * 1024 * 1024),
        )(noisy_luma, scene_cuts)

    return jax.shard_map(
        body,
        mesh=mesh,
        in_specs=(P(("film", "tm"), "rows", "cols"), P("film")),
        out_specs=P(("film", "tm"), "rows", "cols"),
        check_vma=False,
    )
```

```python
import functools

import jax
import jax.numpy as jnp
from jax import lax
from jax.experimental import pallas as pl
from jax.experimental.pallas import tpu as pltpu
from jax.sharding import PartitionSpec as P

MESH = pl.DeviceIdType.MESH

dual_step = 12.0 ** (-0.5)
primal_step = 12.0 ** (-0.5)
radius = 0.6

reach = radius / dual_step
keep = 1.0 / (1.0 + primal_step)
push = primal_step * dual_step / (1.0 + primal_step)
pull = primal_step / (1.0 + primal_step)

TILE = 8
LANES = 128
DEEP = 4


def kernel(tm_size, row_size, x, cuts, out, noisy, relaxed, far, current, dual_t, dual_h, dual_w,
           mask_h, mask_w, load_sem, z_send, z_recv, h_send, h_recv, out_sem):
    frames, rows, cols = x.shape
    high = rows + TILE
    wide = cols + LANES
    split = 3 * (rows // TILE) // 4
    tm = lax.axis_index("tm")
    band = lax.axis_index("rows")
    core = lax.axis_index("cols")
    has_left = tm > 0
    has_right = tm < tm_size - 1
    has_up = band > 0
    has_down = band < row_size - 1
    other = 1 - core
    own_rows = pl.ds(0, rows)
    own_cols = pl.ds(0, cols)

    def at(level, t):
        if level == 0:
            return noisy.at[t + 2]
        if -1 <= t <= frames:
            return relaxed.at[level - 1, t + 1]
        return far.at[2 * (level - 1) + (0 if t < 0 else 1)]

    for ref in (noisy, far):
        for f in range(ref.shape[0]):
            ref[f, rows:high, :] = jnp.zeros((TILE, wide), jnp.float32)

    barrier = pltpu.get_barrier_semaphore()

    def greet(device):
        pl.semaphore_signal(barrier, inc=1, device_id=device, device_id_type=MESH)

    greet({"cols": other})

    @pl.when(has_up)
    def _():
        greet({"rows": band - 1})
        greet({"rows": band - 1, "cols": other})

    @pl.when(has_down)
    def _():
        greet({"rows": band + 1})
        greet({"rows": band + 1, "cols": other})

    @pl.when(has_left)
    def _():
        greet({"tm": tm - 1})

    @pl.when(has_right)
    def _():
        greet({"tm": tm + 1})

    load = pltpu.make_async_copy(x, noisy.at[pl.ds(2, frames), own_rows, own_cols], load_sem)
    load.start()
    count = lambda flag: flag.astype(jnp.int32)
    pl.semaphore_wait(barrier, 1 + 2 * count(has_up) + 2 * count(has_down) + count(has_left) + count(has_right))

    cut = split * TILE
    parts = {3: pl.ds(0, cut), 4: pl.ds(cut, rows - cut)}

    def along_tm(stage):
        part = parts.get(stage, own_rows)
        if stage == 0:
            ends = (x.at[0], at(0, frames)), (x.at[frames - 1], at(0, -1))
        elif stage == 1:
            ends = (x.at[1], at(0, frames + 1)), (x.at[frames - 2], at(0, -2))
        else:
            level = min(stage, 3) - 1
            ends = (
                (at(level, 1).at[part, own_cols], at(level, frames + 1)),
                (at(level, frames - 2).at[part, own_cols], at(level, -2)),
            )
        return [
            pltpu.make_async_remote_copy(
                src_ref=source,
                dst_ref=target.at[part, own_cols],
                send_sem=z_send.at[stage, side],
                recv_sem=z_recv.at[stage, side],
                device_id={"tm": tm - 1 if side == 0 else tm + 1},
                device_id_type=MESH,
            )
            for side, (source, target) in enumerate(ends)
        ]

    def send_frames(stage):
        left, right = along_tm(stage)
        pl.when(has_left)(left.start)
        pl.when(has_right)(right.start)

    def await_frames(stage):
        left, right = along_tm(stage)
        pl.when(has_right)(left.wait_recv)
        pl.when(has_left)(right.wait_recv)

    def await_sent(stage):
        left, right = along_tm(stage)
        pl.when(has_left)(left.wait_send)
        pl.when(has_right)(right.wait_send)

    edge = pl.ds(pl.multiple_of(other * (cols - LANES), LANES), LANES)
    beyond = pl.ds(cols, LANES)
    below, above = pl.ds(rows, DEEP), pl.ds(rows + DEEP, DEEP)
    first, last = pl.ds(0, DEEP), pl.ds(rows - DEEP, DEEP)

    def halo(slot, source, target, lead=(), stage=None):
        def copy(n, src, dst, device):
            return pltpu.make_async_remote_copy(
                src_ref=source.at[lead_src + src], dst_ref=target.at[lead + dst],
                send_sem=h_send.at[slot, n], recv_sem=h_recv.at[slot, n],
                device_id=device, device_id_type=MESH)

        lead_src = (slice(None),) if lead else ()
        ups = [
            copy(0, (first, own_cols), (below, own_cols), {"rows": band - 1}),
            copy(1, (first, edge), (below, beyond), {"rows": band - 1, "cols": other}),
        ]
        downs = [
            copy(2, (last, own_cols), (above, own_cols), {"rows": band + 1}),
            copy(3, (last, edge), (above, beyond), {"rows": band + 1, "cols": other}),
        ]
        part = parts.get(stage, own_rows)
        side = copy(5 if stage == 4 else 4, (part, edge), (part, beyond), {"cols": other})
        return [] if stage == 4 else ups, [] if stage == 3 else downs, side

    def halo_start(copies):
        ups, downs, side = copies
        side.start()

        @pl.when(has_up)
        def _():
            for c in ups:
                c.start()

        @pl.when(has_down)
        def _():
            for c in downs:
                c.start()

    def halo_wait_recv(copies):
        ups, downs, side = copies
        side.wait_recv()

        @pl.when(has_down)
        def _():
            for c in ups:
                c.wait_recv()

        @pl.when(has_up)
        def _():
            for c in downs:
                c.wait_recv()

    def halo_wait_send(copies):
        ups, downs, side = copies
        side.wait_send()

        @pl.when(has_up)
        def _():
            for c in ups:
                c.wait_send()

        @pl.when(has_down)
        def _():
            for c in downs:
                c.wait_send()

    own_halo = halo(0, x, noisy, (pl.ds(2, frames),))

    def halos(stage):
        if stage == 0:
            arrived = at(0, frames), at(0, -1)
        elif stage == 1:
            arrived = at(0, frames + 1), at(0, -2)
        else:
            arrived = at(min(stage, 3) - 1, frames + 1), at(min(stage, 3) - 1, -2)
        return [halo(1 + 2 * min(stage, 3) + side, frame, frame, (), stage) for side, frame in enumerate(arrived)]

    total_frames = frames * tm_size

    def frame_mask(t):
        g = tm * frames + t
        open_ = (g >= 0) & (g <= total_frames - 2)
        for j in range(cuts.shape[0]):
            open_ = open_ & (cuts[j] != g + 1)
        return jnp.where(open_, 1.0, 0.0).astype(jnp.float32)

    frame_masks = {t: frame_mask(t) for t in range(-2, frames + 1)}
    sub = lax.broadcasted_iota(jnp.int32, (TILE, wide), 0)
    first_row = sub == 0
    last_row = sub == TILE - 1

    count_own = rows // TILE

    def dual(level, t, tiles=range(count_own + 1)):
        here, after = at(level - 1, t), at(level - 1, t + 1)
        for i in (tile * TILE for tile in tiles):
            r, n = pl.ds(i, TILE), pl.ds((i + TILE) % high, TILE)
            v = here[r, :]
            a = (after[r, :] - v) * frame_masks[t]
            b = pltpu.roll(jnp.where(first_row, here[n, :], v), TILE - 1, 0) - v
            if i >= rows - TILE:
                b = b * mask_h[pl.ds(i - rows + TILE, TILE), :]
            c = (pltpu.roll(v, wide - 1, 1) - v) * mask_w[...]
            if level > 1:
                a = a + dual_t[t + 2, r, :]
                b = b + dual_h[t + 2, r, :]
                c = c + dual_w[t + 2, r, :]
            shrink = jnp.minimum(1.0, reach * lax.rsqrt(a * a + b * b + c * c))
            dual_t[t + 2, r, :] = a * shrink
            dual_h[t + 2, r, :] = b * shrink
            dual_w[t + 2, r, :] = c * shrink

    def primal(level, t, tiles=None):
        if tiles is None:
            tiles = range(count_own if level == 4 else count_own + 1)
        held = current.at[t + 1]
        start = noisy.at[t + 2]
        before = start if level == 1 else held
        for i in (tile * TILE for tile in tiles):
            r, p = pl.ds(i, TILE), pl.ds((i - TILE) % high, TILE)
            h = dual_h[t + 2, r, :]
            w = dual_w[t + 2, r, :]
            gone = dual_t[t + 2, r, :] - dual_t[t + 1, r, :]
            gone = gone + (h - pltpu.roll(jnp.where(last_row, dual_h[t + 2, p, :], h), 1, 0))
            gone = gone + (w - pltpu.roll(w, 1, 1))
            old = before[r, :]
            new = keep * old + push * gone + pull * start[r, :]
            held[r, :] = new
            if level < 4:
                at(level, t)[r, :] = 2.0 * new - old

    def finish(t):
        return pltpu.make_async_copy(current.at[t + 1, own_rows, own_cols], out.at[t], out_sem.at[t])

    send_frames(0)
    halo_start(own_halo)
    send_frames(1)
    lane = lax.broadcasted_iota(jnp.int32, (TILE, wide), 1)
    mask_w[...] = jnp.where(lane == jnp.where(core == 0, wide - 1, cols - 1), 0.0, 1.0).astype(jnp.float32)
    mask_h[0:TILE, :] = jnp.where(last_row & jnp.logical_not(has_down), 0.0, 1.0).astype(jnp.float32)
    mask_h[TILE : 2 * TILE, :] = jnp.where(last_row & jnp.logical_not(has_up), 0.0, 1.0).astype(jnp.float32)

    def clear(refs):
        def step(i, _):
            r = pl.ds(pl.multiple_of(i * TILE, TILE), TILE)
            for ref in refs:
                ref[r, own_cols] = jnp.zeros((TILE, cols), jnp.float32)
            return 0

        lax.fori_loop(0, rows // TILE, step, 0)

    @pl.when(jnp.logical_not(has_left))
    def _():
        clear([at(0, -1), at(0, -2), at(1, -2), at(2, -2)])

    @pl.when(jnp.logical_not(has_right))
    def _():
        clear([at(0, frames), at(0, frames + 1), at(1, frames + 1), at(2, frames + 1)])

    load.wait()
    halo_wait_recv(own_halo)

    def forward(stage):
        await_frames(stage)
        for copies in halos(stage):
            halo_start(copies)

    def receive(stage):
        for copies in halos(stage):
            halo_wait_recv(copies)

    dual(1, 0)
    dual(1, 1)
    primal(1, 1)
    dual(1, 2)
    primal(1, 2)
    send_frames(2)
    forward(0)
    dual(2, 1)
    receive(0)

    dual(1, -1)
    primal(1, 0)
    dual(1, 3)
    primal(1, 3)
    dual(2, 0)
    primal(2, 1)
    dual(2, 2)
    primal(2, 2)
    send_frames(3)
    send_frames(4)
    forward(1)
    dual(3, 1)
    receive(1)

    dual(1, -2)
    primal(1, -1)
    dual(1, 4)
    primal(1, 4)
    dual(2, -1)
    primal(2, 0)
    dual(2, 3)
    primal(2, 3)
    dual(3, 0)
    primal(3, 1)
    dual(3, 2)
    primal(3, 2)
    forward(2)
    dual(4, 1)
    receive(2)

    dual(2, -2)
    primal(2, -1)
    dual(2, 4)
    primal(2, 4)
    dual(3, -1)
    primal(3, 0)
    dual(3, 3)
    primal(3, 3)
    dual(4, 0)
    primal(4, 1)
    finish(1).start()
    forward(3)
    dual(4, 2)
    primal(4, 2)
    finish(2).start()
    receive(3)

    k, n = split, count_own
    for late in (False, True):
        if late:
            forward(4)
            receive(4)
            duals, primals = [*range(k - 1, n + 1)], [*range(k - 1, n + 1), 0]
            last_duals, last_primals = [*range(k - 2, n + 1), 0], [*range(k - 2, n), 0, 1]
        else:
            duals, primals = range(k - 1), range(1, k - 1)
            last_duals, last_primals = range(1, k - 2), range(2, k - 2)
        dual(3, -2, duals)
        primal(3, -1, primals)
        dual(4, -1, last_duals)
        primal(4, 0, last_primals)
        if late:
            finish(0).start()
        dual(3, 4, duals)
        primal(3, 4, primals)
        dual(4, 3, last_duals)
        primal(4, 3, last_primals)
        if late:
            finish(3).start()

    for stage in range(5):
        await_sent(stage)
        for copies in halos(stage):
            halo_wait_send(copies)
    halo_wait_send(own_halo)
    for t in range(frames):
        finish(t).wait()


def solution(mesh):
    tm_size, row_size = mesh.shape["tm"], mesh.shape["rows"]

    def body(noisy_luma, scene_cuts):
        frames, rows, cols = noisy_luma.shape
        field = (rows + TILE, cols + LANES)
        buffer = lambda *lead: pltpu.VMEM(lead + field, jnp.float32)
        dma = pltpu.SemaphoreType.DMA
        return pl.pallas_call(
            functools.partial(kernel, tm_size, row_size),
            out_shape=jax.ShapeDtypeStruct(noisy_luma.shape, jnp.float32),
            in_specs=[pl.BlockSpec(memory_space=pl.ANY), pl.BlockSpec(memory_space=pltpu.SMEM)],
            out_specs=pl.BlockSpec(memory_space=pl.ANY),
            scratch_shapes=[
                buffer(frames + 4),
                buffer(3, frames + 2),
                buffer(4),
                buffer(frames + 2),
                buffer(frames + 3),
                buffer(frames + 3),
                buffer(frames + 3),
                pltpu.VMEM((2 * TILE, cols + LANES), jnp.float32),
                pltpu.VMEM((TILE, cols + LANES), jnp.float32),
                dma(()),
                dma((5, 2)),
                dma((5, 2)),
                dma((9, 6)),
                dma((9, 6)),
                dma((frames,)),
            ],
            compiler_params=pltpu.CompilerParams(
                collective_id=0, has_side_effects=True, vmem_limit_bytes=48 * 1024 * 1024),
        )(noisy_luma, scene_cuts)

    return jax.shard_map(
        body,
        mesh=mesh,
        in_specs=(P(("film", "tm"), "rows", "cols"), P("film")),
        out_specs=P(("film", "tm"), "rows", "cols"),
        check_vma=False,
    )
```
